32 devices in a mesh: groups: 2 (over y), ctx: 4 (over z), tp: 2 (over x), dp: 2 (over core).
Axes of the slice: x: 2, y: 2, z: 4, core: 2. Of those that a mesh axis runs over, the one named last changes fastest.
Arguments:
- queries: bfloat16 [4, 1024, 4096], P(('groups', 'dp'), 'ctx', 'tp'), parts along dimension 0, may hold values from -27 to 27
- keys_values: bfloat16 [4, 2, 1024, 512], P(('groups', 'dp'), None, ('ctx', 'tp')), parts along dimension 0, may hold values from -9 to 9
- segment_ids: int32 [4, 1024], P(('groups', 'dp'), 'ctx'), parts along dimension 0, may hold values from 0 to 2, as said below
Outputs:
- attended: bfloat16 [4, 1024, 4096], P(('groups', 'dp'), 'ctx', 'tp'), parts along dimension 0
The draws below stay inside these ranges and needn't reach their ends.
There are 2 independent parts, one for each index of `groups`. The reference program is written for one: setup_inputs(seed, part) draws one part's arguments, and reference() takes and returns one part's arrays. A program takes and returns all parts, laid end to end along the dimension named above; each array names one. Nothing has to cross between parts.
Inputs may be any that keep to these rules, and one draw needn't show every extreme that they name: `segment_ids`: ids never fall along rows; the rows of the first 3 indices of ctx form one trajectory with id 0; the rows of every other index of ctx hold one or two whole trajectories, the last index two.
All inputs are finite; a program needn't handle non-finite values.
Results may differ from the reference program's by a relative error of at most 0.0026.
Values may be sent and summed in bfloat16 or wider, within the bound.
A program may use at most 64 MiB of HBM per device.

```python
import math
import jax
import jax.numpy as jnp
from jax import lax

HEAD_DIM = 128
Q_HEADS = 32
KV_HEADS = 4
ROWS_DEV = 256
ROWS = 1024
LONG_DEVS = 3
N_CTX = 4
N_DP = 2


def draw_queries(key, part):
    key = jax.random.fold_in(key, 1)
    shape = (N_DP, ROWS, Q_HEADS, HEAD_DIM)
    values = 1.7 * jnp.clip(jax.random.normal(key, shape, jnp.float32), -5.0, 5.0)
    return values.reshape(N_DP, ROWS, Q_HEADS * HEAD_DIM).astype(jnp.bfloat16)


def draw_keys_values(key, part):
    key = jax.random.fold_in(key, 2)
    value_key = jax.random.fold_in(key, 7)
    shape = (N_DP, ROWS, KV_HEADS, HEAD_DIM)
    key_rows = 1.7 * jnp.clip(jax.random.normal(jax.random.fold_in(key, 11), shape, jnp.float32), -5.0, 5.0)
    value_rows = jnp.clip(jax.random.normal(value_key, shape, jnp.float32), -6.0, 6.0)
    stacked = jnp.stack([key_rows, value_rows], axis=1)
    return stacked.reshape(N_DP, 2, ROWS, KV_HEADS * HEAD_DIM).astype(jnp.bfloat16)


def draw_segment_ids(key, part):
    key = jax.random.fold_in(key, 3)
    rank_list = jnp.arange(N_CTX, dtype=jnp.int32)
    second_one = jax.random.randint(jax.random.fold_in(key, 1), (N_DP, N_CTX), 0, 2)
    second_one = jnp.where(rank_list[None, :] == N_CTX - 1, 1, second_one)
    cut_row = jax.random.randint(jax.random.fold_in(key, 2), (N_DP, N_CTX), ROWS_DEV // 8, ROWS_DEV - ROWS_DEV // 8 + 1)
    row_index = jnp.arange(ROWS, dtype=jnp.int32)
    rank_index = row_index // ROWS_DEV
    within = row_index % ROWS_DEV
    second = (within[None, :] >= cut_row[:, rank_index]).astype(jnp.int32) * second_one[:, rank_index]
    short_id = 1 + 2 * (rank_index[None, :] - LONG_DEVS) + second
    return jnp.where(rank_index[None, :] < LONG_DEVS, 0, short_id).astype(jnp.int32)


def setup_inputs(seed: int = 0, part: int = 0) -> dict:
    keys = jax.random.split(jax.random.key(seed), 4)
    own_keys = jax.random.split(jax.random.fold_in(keys[3], part), 4)
    return {
        "queries": draw_queries(jax.random.fold_in(jax.random.fold_in(keys[3], part), 71), part),
        "keys_values": draw_keys_values(jax.random.fold_in(jax.random.fold_in(keys[3], part), 71), part),
        "segment_ids": draw_segment_ids(jax.random.fold_in(jax.random.fold_in(keys[3], part), 71), part),
    }


def reference(queries, keys_values, segment_ids):
    group_size = Q_HEADS // KV_HEADS
    block_rows = math.gcd(ROWS, 512)
    block_count = ROWS // block_rows
    score_scale = 1.0 / math.sqrt(HEAD_DIM)
    row_index = jnp.arange(ROWS, dtype=jnp.int32)
    batches = []
    for replica in range(N_DP):
        segments = segment_ids[replica]
        head_outputs = []
        for kv_head in range(KV_HEADS):
            key_rows = keys_values[replica, 0, :, kv_head * HEAD_DIM:(kv_head + 1) * HEAD_DIM].astype(jnp.float32)
            value_rows = keys_values[replica, 1, :, kv_head * HEAD_DIM:(kv_head + 1) * HEAD_DIM].astype(jnp.float32)
            grouped = queries[replica, :, kv_head * group_size * HEAD_DIM:(kv_head + 1) * group_size * HEAD_DIM]
            grouped = grouped.reshape(block_count, block_rows, group_size, HEAD_DIM)

            def attend_block(inputs):
                query_block, segment_block, position_block = inputs
                scores = jnp.einsum('qhd,kd->hqk', query_block.astype(jnp.float32), key_rows) * score_scale
                visible = (segment_block[:, None] == segments[None, :]) & (row_index[None, :] <= position_block[:, None])
                scores = jnp.where(visible[None], scores, -1e+30)
                row_top = lax.optimization_barrier(jnp.max(scores, axis=-1, keepdims=True))
                weights = jnp.where(visible[None], jnp.exp(scores - row_top), 0.0)
                totals = lax.optimization_barrier(jnp.sum(weights, axis=-1, keepdims=True))
                rounded = weights.astype(jnp.bfloat16)
                summed = jnp.einsum('hqk,kd->hqd', rounded.astype(jnp.float32), value_rows)
                result = (summed / totals).astype(jnp.bfloat16)
                return jnp.transpose(result, (1, 0, 2)).reshape(block_rows, group_size * HEAD_DIM)
            blocks = lax.map(attend_block, (grouped, segments.reshape(block_count, block_rows), row_index.reshape(block_count, block_rows)))
            head_outputs.append(blocks.reshape(ROWS, group_size * HEAD_DIM))
        batches.append(jnp.concatenate(head_outputs, axis=-1))
    return jnp.stack(batches, axis=0)
```

```python
import functools
import math

import jax
import jax.numpy as jnp
from jax import lax
from jax.experimental import pallas as pl
from jax.experimental.pallas import tpu as pltpu
from jax.sharding import PartitionSpec as P

HEAD_DIM = 128
MESH = pl.DeviceIdType.MESH
LOG2_SCALE = math.log2(math.e) / math.sqrt(HEAD_DIM)


def kernel(n_long, n_tp, q_ref, kv_ref, seg_ref, out_ref, q_v, kv_v, bias_v, top_v, total_v, sum_v, out_v,
           send_sem, recv_sem, q_sem, out_sem):
    groups = kv_v.shape[2]
    rows = q_v.shape[0]
    part = kv_ref.shape[2]
    heads = q_v.shape[1] // HEAD_DIM
    per_group = heads // groups
    width = per_group * HEAD_DIM

    c = lax.axis_index("ctx")
    t = lax.axis_index("tp")
    is_long = c < n_long
    first = jnp.where(is_long, 0, c)
    end = jnp.where(is_long, n_long, c + 1)
    own = jnp.where(is_long, c, 0)

    def q_copy(g):
        columns = pl.ds(g * width, width)
        return pltpu.make_async_copy(q_ref.at[0, :, columns], q_v.at[:, columns], q_sem.at[g])

    def out_copy(g):
        columns = pl.ds(g * width, width)
        return pltpu.make_async_copy(out_v.at[:, columns], out_ref.at[0, :, columns], out_sem.at[g])

    def partner(o):
        return lax.rem(t + o, n_tp)

    def place(g, kv):
        return kv_v.at[own, kv, g, pl.ds(pl.multiple_of(t * part, part), part), :]

    def block(tp_index, g, kv):
        column = pl.multiple_of((tp_index * groups + g) * HEAD_DIM, HEAD_DIM)
        return kv_ref.at[0, kv, :, pl.ds(column, HEAD_DIM)]

    def local_copy(g, kv):
        return pltpu.make_async_copy(block(t, g, kv), place(g, kv), recv_sem.at[own, g, kv])

    def remote_copy(dest, distance, o, g, kv):
        return pltpu.make_async_remote_copy(
            src_ref=block(partner(o), g, kv),
            dst_ref=place(g, kv),
            send_sem=send_sem.at[distance, o, g, kv],
            recv_sem=recv_sem.at[own, g, kv],
            device_id={"ctx": dest, "tp": partner(o)},
            device_id_type=MESH,
        )

    barrier = pltpu.get_barrier_semaphore()
    for o in range(1, n_tp):
        pl.semaphore_signal(barrier, inc=1, device_id={"ctx": c, "tp": partner(o)}, device_id_type=MESH)

    def greet(source, carry):
        for o in range(n_tp):
            pl.semaphore_signal(barrier, inc=1, device_id={"ctx": source, "tp": partner(o)}, device_id_type=MESH)
        return carry

    lax.fori_loop(first, c, greet, 0)
    for g in range(groups):
        for kv in range(2):
            local_copy(g, kv).start()
        q_copy(g).start()
    pl.semaphore_wait(barrier, (end - c) * n_tp - 1)

    for g in range(groups):
        for kv in range(2):
            for o in range(1, n_tp):
                remote_copy(c, 0, o, g, kv).start()
    for g in range(groups):
        for kv in range(2):
            def send(i, carry, g=g, kv=kv):
                dest = end - 1 - i
                for o in range(n_tp):
                    remote_copy(dest, dest - c, o, g, kv).start()
                return carry

            lax.fori_loop(0, end - 1 - c, send, 0)

    seg = seg_ref[...]
    seg_rows = jnp.transpose(jnp.broadcast_to(seg.astype(jnp.float32), (HEAD_DIM, rows)))[:, :1].astype(jnp.int32)
    row_index = lax.broadcasted_iota(jnp.int32, (rows, rows), 0)
    key_index = lax.broadcasted_iota(jnp.int32, (rows, rows), 1)
    visible = (seg_rows == seg) & (key_index <= row_index)
    bias_v[...] = jnp.where(visible, 0.0, -1e30)

    def arrived(slot, g, kv):
        whole = kv_v.at[slot, kv, g]
        pltpu.make_async_copy(whole, whole, recv_sem.at[slot, g, kv]).wait()

    def scores_of(h, key_rows):
        q = q_v[:, pl.ds(pl.multiple_of(h * HEAD_DIM, HEAD_DIM), HEAD_DIM)]
        return lax.dot_general(q, key_rows, (((1,), (1,)), ((), ())), preferred_element_type=jnp.float32) * LOG2_SCALE

    for g in range(groups):
        q_copy(g).wait()
        arrived(own, g, 0)
        arrived(own, g, 1)

        def own_head(i, carry, g=g):
            h = g * per_group + i
            scores = scores_of(h, kv_v[own, 0, g]) + bias_v[...]
            top = jnp.max(scores, axis=1, keepdims=True)
            weights = jnp.exp2(scores - top)
            top_v[h] = jnp.broadcast_to(top, (rows, HEAD_DIM))
            total_v[h] = jnp.broadcast_to(jnp.sum(weights, axis=1, keepdims=True), (rows, HEAD_DIM))
            sum_v[h] = jnp.dot(weights.astype(jnp.bfloat16), kv_v[own, 1, g], preferred_element_type=jnp.float32)
            return carry

        lax.fori_loop(0, per_group, own_head, 0, unroll=2)

    for g in range(groups):
        def source_step(i, carry, g=g):
            slot = c - 1 - i
            arrived(slot, g, 0)
            arrived(slot, g, 1)

            def head(j, inner):
                h = g * per_group + j
                scores = scores_of(h, kv_v[slot, 0, g])
                old = top_v[h]
                top = jnp.maximum(old, jnp.max(scores, axis=1, keepdims=True))
                weights = jnp.exp2(scores - top[:, :1])
                factor = jnp.exp2(old - top)
                top_v[h] = top
                total_v[h] = total_v[h] * factor + jnp.sum(weights, axis=1, keepdims=True)
                sum_v[h] = sum_v[h] * factor + jnp.dot(
                    weights.astype(jnp.bfloat16), kv_v[slot, 1, g], preferred_element_type=jnp.float32
                )
                return inner

            return lax.fori_loop(0, per_group, head, carry, unroll=2)

        lax.fori_loop(0, c - first, source_step, 0)

        def finish(j, carry, g=g):
            h = g * per_group + j
            columns = pl.ds(pl.multiple_of(h * HEAD_DIM, HEAD_DIM), HEAD_DIM)
            out_v[:, columns] = (sum_v[h] / total_v[h]).astype(jnp.bfloat16)
            return carry

        lax.fori_loop(0, per_group, finish, 0)
        out_copy(g).start()

    for g in range(groups):
        for kv in range(2):
            for o in range(1, n_tp):
                remote_copy(c, 0, o, g, kv).wait_send()

            def sent(i, carry, g=g, kv=kv):
                for o in range(n_tp):
                    remote_copy(c + 1 + i, 1 + i, o, g, kv).wait_send()
                return carry

            lax.fori_loop(0, end - 1 - c, sent, 0)
    for g in range(groups):
        out_copy(g).wait()


def per_device(n_long, n_tp, queries, keys_values, segment_ids):
    rows, columns = queries.shape[1:]
    heads = columns // HEAD_DIM
    groups = keys_values.shape[3] // HEAD_DIM // n_tp
    return pl.pallas_call(
        functools.partial(kernel, n_long, n_tp),
        out_shape=jax.ShapeDtypeStruct(queries.shape, queries.dtype),
        in_specs=[
            pl.BlockSpec(memory_space=pl.ANY),
            pl.BlockSpec(memory_space=pl.ANY),
            pl.BlockSpec(memory_space=pltpu.VMEM),
        ],
        out_specs=pl.BlockSpec(memory_space=pl.ANY),
        scratch_shapes=[
            pltpu.VMEM((rows, columns), jnp.bfloat16),
            pltpu.VMEM((n_long, 2, groups, rows, HEAD_DIM), jnp.bfloat16),
            pltpu.VMEM((rows, rows), jnp.float32),
            pltpu.VMEM((heads, rows, HEAD_DIM), jnp.float32),
            pltpu.VMEM((heads, rows, HEAD_DIM), jnp.float32),
            pltpu.VMEM((heads, rows, HEAD_DIM), jnp.float32),
            pltpu.VMEM((rows, columns), jnp.bfloat16),
            pltpu.SemaphoreType.DMA((n_long, n_tp, groups, 2)),
            pltpu.SemaphoreType.DMA((n_long, groups, 2)),
            pltpu.SemaphoreType.DMA((groups,)),
            pltpu.SemaphoreType.DMA((groups,)),
        ],
        compiler_params=pltpu.CompilerParams(
            collective_id=0, has_side_effects=True, vmem_limit_bytes=32 * 1024 * 1024
        ),
    )(queries, keys_values, segment_ids)


def solution(mesh):
    n_long = mesh.shape["ctx"] // 2 + 1
    return jax.shard_map(
        functools.partial(per_device, n_long, mesh.shape["tp"]),
        mesh=mesh,
        in_specs=(
            P(("groups", "dp"), "ctx", "tp"),
            P(("groups", "dp"), None, ("ctx", "tp"), None),
            P(("groups", "dp"), "ctx"),
        ),
        out_specs=P(("groups", "dp"), "ctx", "tp"),
        check_vma=False,
    )
```

```python
import functools
import math

import jax
import jax.numpy as jnp
from jax import lax
from jax.experimental import pallas as pl
from jax.experimental.pallas import tpu as pltpu
from jax.sharding import PartitionSpec as P

HEAD_DIM = 128
MESH = pl.DeviceIdType.MESH
LOG2_SCALE = math.log2(math.e) / math.sqrt(HEAD_DIM)


def kernel(n_long, n_tp, q_ref, kv_ref, seg_ref, out_ref, q_v, kv_v, bias_v, flip_v, top_v, total_v, sum_v, out_v,
           send_sem, recv_sem, q_sem, out_sem):
    groups = kv_v.shape[2]
    rows = q_v.shape[0]
    part = kv_ref.shape[2]
    heads = q_v.shape[1] // HEAD_DIM
    per_group = heads // groups
    width = per_group * HEAD_DIM

    c = lax.axis_index("ctx")
    t = lax.axis_index("tp")
    is_long = c < n_long
    first = jnp.where(is_long, 0, c)
    end = jnp.where(is_long, n_long, c + 1)
    own = jnp.where(is_long, c, 0)

    def q_copy(g):
        columns = pl.ds(g * width, width)
        return pltpu.make_async_copy(q_ref.at[0, :, columns], q_v.at[:, columns], q_sem.at[g])

    def out_copy(g):
        columns = pl.ds(g * width, width)
        return pltpu.make_async_copy(out_v.at[:, columns], out_ref.at[0, :, columns], out_sem.at[g])

    def partner(o):
        return lax.rem(t + o, n_tp)

    def place(g, kv):
        return kv_v.at[own, kv, g, pl.ds(pl.multiple_of(t * part, part), part), :]

    def block(tp_index, g, kv):
        column = pl.multiple_of((tp_index * groups + g) * HEAD_DIM, HEAD_DIM)
        return kv_ref.at[0, kv, :, pl.ds(column, HEAD_DIM)]

    def local_copy(g, kv):
        return pltpu.make_async_copy(block(t, g, kv), place(g, kv), recv_sem.at[own, g, kv])

    def remote_copy(dest, distance, o, g, kv):
        return pltpu.make_async_remote_copy(
            src_ref=block(partner(o), g, kv),
            dst_ref=place(g, kv),
            send_sem=send_sem.at[distance, o, g, kv],
            recv_sem=recv_sem.at[own, g, kv],
            device_id={"ctx": dest, "tp": partner(o)},
            device_id_type=MESH,
        )

    barrier = pltpu.get_barrier_semaphore()
    for o in range(1, n_tp):
        pl.semaphore_signal(barrier, inc=1, device_id={"ctx": c, "tp": partner(o)}, device_id_type=MESH)

    def greet(source, carry):
        for o in range(n_tp):
            pl.semaphore_signal(barrier, inc=1, device_id={"ctx": source, "tp": partner(o)}, device_id_type=MESH)
        return carry

    lax.fori_loop(first, c, greet, 0)
    for g in range(groups):
        for kv in range(2):
            local_copy(g, kv).start()
        q_copy(g).start()
    pl.semaphore_wait(barrier, (end - c) * n_tp - 1)

    for g in range(groups):
        for kv in range(2):
            for o in range(1, n_tp):
                remote_copy(c, 0, o, g, kv).start()
    for g in range(groups):
        for kv in range(2):
            def send(i, carry, g=g, kv=kv):
                dest = end - 1 - i
                for o in range(n_tp):
                    remote_copy(dest, dest - c, o, g, kv).start()
                return carry

            lax.fori_loop(0, end - 1 - c, send, 0)

    seg = seg_ref[...]
    seg_keys = jnp.transpose(jnp.broadcast_to(seg.astype(jnp.float32), (HEAD_DIM, rows)))[:, :1].astype(jnp.int32)
    key_index = lax.broadcasted_iota(jnp.int32, (rows, rows), 0)
    row_index = lax.broadcasted_iota(jnp.int32, (rows, rows), 1)
    visible = (seg_keys == seg) & (key_index <= row_index)
    bias_v[...] = jnp.where(visible, 0.0, -1e30)

    def arrived(slot, g, kv):
        whole = kv_v.at[slot, kv, g]
        pltpu.make_async_copy(whole, whole, recv_sem.at[slot, g, kv]).wait()

    def scores_of(h, key_rows):
        q = q_v[:, pl.ds(pl.multiple_of(h * HEAD_DIM, HEAD_DIM), HEAD_DIM)]
        return lax.dot_general(key_rows, q, (((1,), (1,)), ((), ())), preferred_element_type=jnp.float32) * LOG2_SCALE

    def attend(g, slot, bias, fresh):
        key_rows = kv_v[slot, 0, g]
        flip_v[...] = jnp.transpose(kv_v[slot, 1, g])
        heads_of = [g * per_group + j for j in range(per_group)]

        def add_values(h, weights, factor):
            product = jnp.dot(flip_v[...], weights, preferred_element_type=jnp.float32)
            sum_v[h] = product if fresh else sum_v[h] * factor + product

        scores, waiting = scores_of(heads_of[0], key_rows), None
        for j, h in enumerate(heads_of):
            following = scores_of(heads_of[j + 1], key_rows) if j + 1 < per_group else None
            if bias is not None:
                scores = scores + bias[...]
            top = jnp.max(scores, axis=0, keepdims=True)
            factor = None
            if not fresh:
                old = top_v[h]
                top = jnp.maximum(old, top)
                factor = jnp.exp2(old - top)
            weights = jnp.exp2(scores - top)
            total = jnp.sum(weights, axis=0, keepdims=True)
            top_v[h] = top
            total_v[h] = total if fresh else total_v[h] * factor + total
            if waiting is not None:
                add_values(*waiting)
            waiting = (h, weights.astype(jnp.bfloat16), factor)
            scores = following
        add_values(*waiting)

    for g in range(groups):
        q_copy(g).wait()
        arrived(own, g, 0)
        arrived(own, g, 1)
        attend(g, own, bias_v, True)

    for g in range(groups):
        def source_step(i, carry, g=g):
            slot = c - 1 - i
            arrived(slot, g, 0)
            arrived(slot, g, 1)
            attend(g, slot, None, False)
            return carry

        lax.fori_loop(0, c - first, source_step, 0)

        def finish(j, carry, g=g):
            h = g * per_group + j
            columns = pl.ds(pl.multiple_of(h * HEAD_DIM, HEAD_DIM), HEAD_DIM)
            out_v[:, columns] = jnp.transpose((sum_v[h] * (1.0 / total_v[h])).astype(jnp.bfloat16))
            return carry

        lax.fori_loop(0, per_group, finish, 0, unroll=2)
        out_copy(g).start()

    for g in range(groups):
        for kv in range(2):
            for o in range(1, n_tp):
                remote_copy(c, 0, o, g, kv).wait_send()

            def sent(i, carry, g=g, kv=kv):
                for o in range(n_tp):
                    remote_copy(c + 1 + i, 1 + i, o, g, kv).wait_send()
                return carry

            lax.fori_loop(0, end - 1 - c, sent, 0)
    for g in range(groups):
        out_copy(g).wait()


def place_result(source_ref, out_ref, held, in_sems, out_sems):
    pieces = in_sems.shape[0]
    size = source_ref.shape[1] // pieces

    def rows_of(i):
        return pl.ds(i * size, size)

    def load(i):
        return pltpu.make_async_copy(source_ref.at[0, rows_of(i)], held.at[rows_of(i)], in_sems.at[i])

    def store(i):
        return pltpu.make_async_copy(held.at[rows_of(i)], out_ref.at[0, rows_of(i)], out_sems.at[i])

    for i in range(pieces):
        load(i).start()
    for i in range(pieces):
        load(i).wait()
        store(i).start()
    for i in range(pieces):
        store(i).wait()


def per_device(n_long, n_tp, queries, keys_values, segment_ids):
    rows, columns = queries.shape[1:]
    heads = columns // HEAD_DIM
    groups = keys_values.shape[3] // HEAD_DIM // n_tp
    attended = pl.pallas_call(
        functools.partial(kernel, n_long, n_tp),
        out_shape=jax.ShapeDtypeStruct(queries.shape, queries.dtype),
        in_specs=[
            pl.BlockSpec(memory_space=pltpu.HBM),
            pl.BlockSpec(memory_space=pltpu.HBM),
            pl.BlockSpec(memory_space=pltpu.VMEM),
        ],
        out_specs=pl.BlockSpec(memory_space=pl.ANY),
        scratch_shapes=[
            pltpu.VMEM((rows, columns), jnp.bfloat16),
            pltpu.VMEM((n_long, 2, groups, rows, HEAD_DIM), jnp.bfloat16),
            pltpu.VMEM((rows, rows), jnp.float32),
            pltpu.VMEM((HEAD_DIM, rows), jnp.bfloat16),
            pltpu.VMEM((heads, 1, rows), jnp.float32),
            pltpu.VMEM((heads, 1, rows), jnp.float32),
            pltpu.VMEM((heads, HEAD_DIM, rows), jnp.float32),
            pltpu.VMEM((rows, columns), jnp.bfloat16),
            pltpu.SemaphoreType.DMA((n_long, n_tp, groups, 2)),
            pltpu.SemaphoreType.DMA((n_long, groups, 2)),
            pltpu.SemaphoreType.DMA((groups,)),
            pltpu.SemaphoreType.DMA((groups,)),
        ],
        compiler_params=pltpu.CompilerParams(
            collective_id=0, has_side_effects=True, vmem_limit_bytes=60 * 1024 * 1024
        ),
    )(queries, keys_values, segment_ids)
    return pl.pallas_call(
        place_result,
        out_shape=jax.ShapeDtypeStruct(queries.shape, queries.dtype),
        in_specs=[pl.BlockSpec(memory_space=pl.ANY)],
        out_specs=pl.BlockSpec(memory_space=pl.ANY),
        scratch_shapes=[
            pltpu.VMEM((rows, columns), queries.dtype),
            pltpu.SemaphoreType.DMA((4,)),
            pltpu.SemaphoreType.DMA((4,)),
        ],
        compiler_params=pltpu.CompilerParams(vmem_limit_bytes=60 * 1024 * 1024),
    )(attended)


def solution(mesh):
    n_long = mesh.shape["ctx"] // 2 + 1
    return jax.shard_map(
        functools.partial(per_device, n_long, mesh.shape["tp"]),
        mesh=mesh,
        in_specs=(
            P(("groups", "dp"), "ctx", "tp"),
            P(("groups", "dp"), None, ("ctx", "tp"), None),
            P(("groups", "dp"), "ctx"),
        ),
        out_specs=P(("groups", "dp"), "ctx", "tp"),
        check_vma=False,
    )
```

```python
import functools
import math

import jax
import jax.numpy as jnp
from jax import lax
from jax.experimental import pallas as pl
from jax.experimental.pallas import tpu as pltpu
from jax.sharding import PartitionSpec as P

HEAD_DIM = 128
MESH = pl.DeviceIdType.MESH
LOG2_SCALE = math.log2(math.e) / math.sqrt(HEAD_DIM)


def kernel(n_long, n_tp, q_ref, kv_ref, seg_ref, out_ref, q_v, seg_v, stage_v, kv_v, bias_v, flip_v, top_v, total_v, sum_v,
           stage_sem, send_sem, recv_sem, q_sem, seg_sem):
    groups = kv_v.shape[2]
    rows = q_v.shape[0]
    part = kv_ref.shape[2]
    heads = q_v.shape[1] // HEAD_DIM
    per_group = heads // groups
    width = per_group * HEAD_DIM

    c = lax.axis_index("ctx")
    t = lax.axis_index("tp")
    is_long = c < n_long
    first = jnp.where(is_long, 0, c)
    end = jnp.where(is_long, n_long, c + 1)
    own = jnp.where(is_long, c, 0)

    def q_copy(g):
        columns = pl.ds(g * width, width)
        return pltpu.make_async_copy(q_ref.at[0, :, columns], q_v.at[:, columns], q_sem.at[g])

    seg_copy = pltpu.make_async_copy(seg_ref, seg_v, seg_sem)

    def partner(o):
        return lax.rem(t + o, n_tp)

    def place(g, kv):
        return kv_v.at[own, kv, g, pl.ds(pl.multiple_of(t * part, part), part), :]

    def block(tp_index, g, kv):
        column = pl.multiple_of((tp_index * groups + g) * HEAD_DIM, HEAD_DIM)
        return kv_ref.at[0, kv, :, pl.ds(column, HEAD_DIM)]

    def stage_copy(tp_index, g, kv):
        return pltpu.make_async_copy(block(tp_index, g, kv), stage_v.at[kv, g, tp_index], stage_sem.at[kv, g, tp_index])

    def local_copy(g, kv):
        return pltpu.make_async_copy(block(t, g, kv), place(g, kv), recv_sem.at[own, g, kv])

    def remote_copy(dest, distance, o, g, kv):
        return pltpu.make_async_remote_copy(
            src_ref=stage_v.at[kv, g, partner(o)],
            dst_ref=place(g, kv),
            send_sem=send_sem.at[distance, o, g, kv],
            recv_sem=recv_sem.at[own, g, kv],
            device_id={"ctx": dest, "tp": partner(o)},
            device_id_type=MESH,
        )

    barrier = pltpu.get_barrier_semaphore()
    for g in range(groups):
        for kv in range(2):
            for i in range(n_tp):
                stage_copy(i, g, kv).start()
    for o in range(1, n_tp):
        pl.semaphore_signal(barrier, inc=1, device_id={"ctx": c, "tp": partner(o)}, device_id_type=MESH)

    def greet(source, carry):
        for o in range(n_tp):
            pl.semaphore_signal(barrier, inc=1, device_id={"ctx": source, "tp": partner(o)}, device_id_type=MESH)
        return carry

    lax.fori_loop(first, c, greet, 0)
    for g in range(groups):
        for kv in range(2):
            local_copy(g, kv).start()
        q_copy(g).start()
    seg_copy.start()
    for g in range(groups):
        for kv in range(2):
            for i in range(n_tp):
                stage_copy(i, g, kv).wait()
    pl.semaphore_wait(barrier, (end - c) * n_tp - 1)

    for g in range(groups):
        for kv in range(2):
            for o in range(1, n_tp):
                remote_copy(c, 0, o, g, kv).start()
    for g in range(groups):
        for kv in range(2):
            def send(i, carry, g=g, kv=kv):
                dest = c + 1 + i
                for o in range(n_tp):
                    remote_copy(dest, dest - c, o, g, kv).start()
                return carry

            lax.fori_loop(0, end - 1 - c, send, 0)

    seg_copy.wait()
    seg = seg_v[...]
    seg_keys = jnp.transpose(jnp.broadcast_to(seg.astype(jnp.float32), (HEAD_DIM, rows)))[:, :1].astype(jnp.int32)
    key_index = lax.broadcasted_iota(jnp.int32, (rows, rows), 0)
    row_index = lax.broadcasted_iota(jnp.int32, (rows, rows), 1)
    visible = (seg_keys == seg) & (key_index <= row_index)
    bias_v[...] = jnp.where(visible, 0.0, -1e30)

    def arrived(slot, g, kv):
        whole = kv_v.at[slot, kv, g]
        pltpu.make_async_copy(whole, whole, recv_sem.at[slot, g, kv]).wait()

    def scores_of(h, key_rows):
        q = q_v[:, pl.ds(pl.multiple_of(h * HEAD_DIM, HEAD_DIM), HEAD_DIM)]
        return lax.dot_general(key_rows, q, (((1,), (1,)), ((), ())), preferred_element_type=jnp.float32) * LOG2_SCALE

    def attend(g, slot, bias, fresh):
        key_rows = kv_v[slot, 0, g]
        flip_v[...] = jnp.transpose(kv_v[slot, 1, g])
        heads_of = [g * per_group + j for j in range(per_group)]

        def add_values(h, weights, factor):
            product = jnp.dot(flip_v[...], weights, preferred_element_type=jnp.float32)
            sum_v[h] = product if fresh else sum_v[h] * factor + product

        scores, waiting = scores_of(heads_of[0], key_rows), None
        for j, h in enumerate(heads_of):
            following = scores_of(heads_of[j + 1], key_rows) if j + 1 < per_group else None
            if bias is not None:
                scores = scores + bias[...]
            top = jnp.max(scores, axis=0, keepdims=True)
            factor = None
            if not fresh:
                old = top_v[h]
                top = jnp.maximum(old, top)
                factor = jnp.exp2(old - top)
            weights = jnp.exp2(scores - top)
            total = jnp.sum(weights, axis=0, keepdims=True)
            top_v[h] = top
            total_v[h] = total if fresh else total_v[h] * factor + total
            if waiting is not None:
                add_values(*waiting)
            waiting = (h, weights.astype(jnp.bfloat16), factor)
            scores = following
        add_values(*waiting)

    for g in range(groups):
        q_copy(g).wait()
        arrived(own, g, 0)
        arrived(own, g, 1)
        attend(g, own, bias_v, True)

    for g in range(groups):
        def source_step(i, carry, g=g):
            slot = c - 1 - i
            arrived(slot, g, 0)
            arrived(slot, g, 1)
            attend(g, slot, None, False)
            return carry

        lax.fori_loop(0, c - first, source_step, 0)

        def finish(j, carry, g=g):
            h = g * per_group + j
            columns = pl.ds(pl.multiple_of(h * HEAD_DIM, HEAD_DIM), HEAD_DIM)
            out_ref[0, :, columns] = jnp.transpose((sum_v[h] * (1.0 / total_v[h])).astype(jnp.bfloat16))
            return carry

        lax.fori_loop(0, per_group, finish, 0, unroll=2)

    for g in range(groups):
        for kv in range(2):
            for o in range(1, n_tp):
                remote_copy(c, 0, o, g, kv).wait_send()

            def sent(i, carry, g=g, kv=kv):
                for o in range(n_tp):
                    remote_copy(c + 1 + i, 1 + i, o, g, kv).wait_send()
                return carry

            lax.fori_loop(0, end - 1 - c, sent, 0)


def per_device(n_long, n_tp, queries, keys_values, segment_ids):
    rows, columns = queries.shape[1:]
    heads = columns // HEAD_DIM
    groups = keys_values.shape[3] // HEAD_DIM // n_tp
    return pl.pallas_call(
        functools.partial(kernel, n_long, n_tp),
        out_shape=pltpu.VMEM(queries.shape, queries.dtype),
        in_specs=[
            pl.BlockSpec(memory_space=pltpu.HBM),
            pl.BlockSpec(memory_space=pltpu.HBM),
            pl.BlockSpec(memory_space=pltpu.HBM),
        ],
        out_specs=pl.BlockSpec(memory_space=pltpu.VMEM),
        scratch_shapes=[
            pltpu.VMEM((rows, columns), jnp.bfloat16),
            pltpu.VMEM((1, rows), jnp.int32),
            pltpu.VMEM((2, groups, n_tp, keys_values.shape[2], HEAD_DIM), jnp.bfloat16),
            pltpu.VMEM((n_long, 2, groups, rows, HEAD_DIM), jnp.bfloat16),
            pltpu.VMEM((rows, rows), jnp.float32),
            pltpu.VMEM((HEAD_DIM, rows), jnp.bfloat16),
            pltpu.VMEM((heads, 1, rows), jnp.float32),
            pltpu.VMEM((heads, 1, rows), jnp.float32),
            pltpu.VMEM((heads, HEAD_DIM, rows), jnp.float32),
            pltpu.SemaphoreType.DMA((2, groups, n_tp)),
            pltpu.SemaphoreType.DMA((n_long, n_tp, groups, 2)),
            pltpu.SemaphoreType.DMA((n_long, groups, 2)),
            pltpu.SemaphoreType.DMA((groups,)),
            pltpu.SemaphoreType.DMA,
        ],
        compiler_params=pltpu.CompilerParams(
            collective_id=0, has_side_effects=True, vmem_limit_bytes=60 * 1024 * 1024
        ),
    )(queries, keys_values, segment_ids)


def solution(mesh):
    n_long = mesh.shape["ctx"] // 2 + 1
    return jax.shard_map(
        functools.partial(per_device, n_long, mesh.shape["tp"]),
        mesh=mesh,
        in_specs=(
            P(("groups", "dp"), "ctx", "tp"),
            P(("groups", "dp"), None, ("ctx", "tp"), None),
            P(("groups", "dp"), "ctx"),
        ),
        out_specs=P(("groups", "dp"), "ctx", "tp"),
        check_vma=False,
    )
```

```python
import functools
import math

import jax
import jax.numpy as jnp
from jax import lax
from jax.experimental import pallas as pl
from jax.experimental.pallas import tpu as pltpu
from jax.sharding import PartitionSpec as P

HEAD_DIM = 128
MESH = pl.DeviceIdType.MESH
LOG2_SCALE = math.log2(math.e) / math.sqrt(HEAD_DIM)


def kernel(n_long, n_tp, q_ref, kv_ref, seg_ref, out_ref, q_v, seg_v, stage_v, kv_v, bias_v, flip_v, top_v, total_v, sum_v, weights_v, factor_v,
           stage_sem, send_sem, recv_sem, q_sem, seg_sem):
    groups = kv_v.shape[2]
    rows = q_v.shape[0]
    part = kv_ref.shape[2]
    heads = q_v.shape[1] // HEAD_DIM
    per_group = heads // groups
    width = per_group * HEAD_DIM

    c = lax.axis_index("ctx")
    t = lax.axis_index("tp")
    is_long = c < n_long
    first = jnp.where(is_long, 0, c)
    end = jnp.where(is_long, n_long, c + 1)
    own = jnp.where(is_long, c, 0)

    def q_copy(g):
        columns = pl.ds(g * width, width)
        return pltpu.make_async_copy(q_ref.at[0, :, columns], q_v.at[:, columns], q_sem.at[g])

    seg_copy = pltpu.make_async_copy(seg_ref, seg_v, seg_sem)

    def partner(o):
        return lax.rem(t + o, n_tp)

    def place(g, kv):
        return kv_v.at[own, kv, g, pl.ds(pl.multiple_of(t * part, part), part), :]

    def block(tp_index, g, kv):
        column = pl.multiple_of((tp_index * groups + g) * HEAD_DIM, HEAD_DIM)
        return kv_ref.at[0, kv, :, pl.ds(column, HEAD_DIM)]

    def stage_copy(tp_index, g, kv):
        return pltpu.make_async_copy(block(tp_index, g, kv), stage_v.at[kv, g, tp_index], stage_sem.at[kv, g, tp_index])

    def local_copy(g, kv):
        return pltpu.make_async_copy(block(t, g, kv), place(g, kv), recv_sem.at[own, g, kv])

    def remote_copy(dest, distance, o, g, kv):
        return pltpu.make_async_remote_copy(
            src_ref=stage_v.at[kv, g, partner(o)],
            dst_ref=place(g, kv),
            send_sem=send_sem.at[distance, o, g, kv],
            recv_sem=recv_sem.at[own, g, kv],
            device_id={"ctx": dest, "tp": partner(o)},
            device_id_type=MESH,
        )

    barrier = pltpu.get_barrier_semaphore()
    for g in range(groups):
        for kv in range(2):
            for i in range(n_tp):
                stage_copy(i, g, kv).start()
    for o in range(1, n_tp):
        pl.semaphore_signal(barrier, inc=1, device_id={"ctx": c, "tp": partner(o)}, device_id_type=MESH)

    def greet(source, carry):
        for o in range(n_tp):
            pl.semaphore_signal(barrier, inc=1, device_id={"ctx": source, "tp": partner(o)}, device_id_type=MESH)
        return carry

    lax.fori_loop(first, c, greet, 0)
    for g in range(groups):
        for kv in range(2):
            local_copy(g, kv).start()
        q_copy(g).start()
    seg_copy.start()
    for g in range(groups):
        for kv in range(2):
            for i in range(n_tp):
                stage_copy(i, g, kv).wait()
    pl.semaphore_wait(barrier, (end - c) * n_tp - 1)

    for g in range(groups):
        for kv in range(2):
            for o in range(1, n_tp):
                remote_copy(c, 0, o, g, kv).start()
    for g in range(groups):
        for kv in range(2):
            def send(i, carry, g=g, kv=kv):
                dest = c + 1 + i
                for o in range(n_tp):
                    remote_copy(dest, dest - c, o, g, kv).start()
                return carry

            lax.fori_loop(0, end - 1 - c, send, 0)

    seg_copy.wait()
    seg = seg_v[...]
    seg_keys = jnp.transpose(jnp.broadcast_to(seg.astype(jnp.float32), (HEAD_DIM, rows)))[:, :1].astype(jnp.int32)
    key_index = lax.broadcasted_iota(jnp.int32, (rows, rows), 0)
    row_index = lax.broadcasted_iota(jnp.int32, (rows, rows), 1)
    visible = (seg_keys == seg) & (key_index <= row_index)
    bias_v[...] = jnp.where(visible, 0.0, -1e30)

    def arrived(slot, g, kv):
        whole = kv_v.at[slot, kv, g]
        pltpu.make_async_copy(whole, whole, recv_sem.at[slot, g, kv]).wait()

    def scores_of(h, key_rows):
        q = q_v[:, pl.ds(pl.multiple_of(h * HEAD_DIM, HEAD_DIM), HEAD_DIM)]
        return lax.dot_general(key_rows, q, (((1,), (1,)), ((), ())), preferred_element_type=jnp.float32) * LOG2_SCALE

    def attend(g, slot, bias, fresh):
        key_rows = kv_v[slot, 0, g]
        if fresh:
            flip_v[...] = jnp.transpose(kv_v[slot, 1, g])
        heads_of = [g * per_group + j for j in range(per_group)]

        def add_values(h, weights, factor):
            product = jnp.dot(flip_v[...], weights, preferred_element_type=jnp.float32)
            sum_v[h] = product if fresh else sum_v[h] * factor + product

        scores, waiting = scores_of(heads_of[0], key_rows), None
        for j, h in enumerate(heads_of):
            following = scores_of(heads_of[j + 1], key_rows) if j + 1 < per_group else None
            if bias is not None:
                scores = scores + bias[...]
            top = jnp.max(scores, axis=0, keepdims=True)
            factor = None
            if not fresh:
                old = top_v[h]
                top = jnp.maximum(old, top)
                factor = jnp.exp2(old - top)
            weights = jnp.exp2(scores - top)
            total = jnp.sum(weights, axis=0, keepdims=True)
            top_v[h] = top
            total_v[h] = total if fresh else total_v[h] * factor + total
            scores = following
            if not fresh:
                weights_v[j] = weights.astype(jnp.bfloat16)
                factor_v[j] = factor
                continue
            if waiting is not None:
                add_values(*waiting)
            waiting = (h, weights.astype(jnp.bfloat16), factor)
        if fresh:
            add_values(*waiting)
            return
        arrived(slot, g, 1)
        flip_v[...] = jnp.transpose(kv_v[slot, 1, g])
        for j, h in enumerate(heads_of):
            add_values(h, weights_v[j], factor_v[j])

    for g in range(groups):
        q_copy(g).wait()
        arrived(own, g, 0)
        arrived(own, g, 1)
        attend(g, own, bias_v, True)

    for g in range(groups):
        def source_step(i, carry, g=g):
            slot = c - 1 - i
            arrived(slot, g, 0)
            attend(g, slot, None, False)
            return carry

        lax.fori_loop(0, c - first, source_step, 0)

        def finish(j, carry, g=g):
            h = g * per_group + j
            columns = pl.ds(pl.multiple_of(h * HEAD_DIM, HEAD_DIM), HEAD_DIM)
            out_ref[0, :, columns] = jnp.transpose((sum_v[h] * (1.0 / total_v[h])).astype(jnp.bfloat16))
            return carry

        lax.fori_loop(0, per_group, finish, 0, unroll=2)

    for g in range(groups):
        for kv in range(2):
            for o in range(1, n_tp):
                remote_copy(c, 0, o, g, kv).wait_send()

            def sent(i, carry, g=g, kv=kv):
                for o in range(n_tp):
                    remote_copy(c + 1 + i, 1 + i, o, g, kv).wait_send()
                return carry

            lax.fori_loop(0, end - 1 - c, sent, 0)


def per_device(n_long, n_tp, queries, keys_values, segment_ids):
    rows, columns = queries.shape[1:]
    heads = columns // HEAD_DIM
    groups = keys_values.shape[3] // HEAD_DIM // n_tp
    return pl.pallas_call(
        functools.partial(kernel, n_long, n_tp),
        out_shape=pltpu.VMEM(queries.shape, queries.dtype),
        in_specs=[
            pl.BlockSpec(memory_space=pltpu.HBM),
            pl.BlockSpec(memory_space=pltpu.HBM),
            pl.BlockSpec(memory_space=pltpu.HBM),
        ],
        out_specs=pl.BlockSpec(memory_space=pltpu.VMEM),
        scratch_shapes=[
            pltpu.VMEM((rows, columns), jnp.bfloat16),
            pltpu.VMEM((1, rows), jnp.int32),
            pltpu.VMEM((2, groups, n_tp, keys_values.shape[2], HEAD_DIM), jnp.bfloat16),
            pltpu.VMEM((n_long, 2, groups, rows, HEAD_DIM), jnp.bfloat16),
            pltpu.VMEM((rows, rows), jnp.float32),
            pltpu.VMEM((HEAD_DIM, rows), jnp.bfloat16),
            pltpu.VMEM((heads, 1, rows), jnp.float32),
            pltpu.VMEM((heads, 1, rows), jnp.float32),
            pltpu.VMEM((heads, HEAD_DIM, rows), jnp.float32),
            pltpu.VMEM((heads // groups, rows, rows), jnp.bfloat16),
            pltpu.VMEM((heads // groups, 1, rows), jnp.float32),
            pltpu.SemaphoreType.DMA((2, groups, n_tp)),
            pltpu.SemaphoreType.DMA((n_long, n_tp, groups, 2)),
            pltpu.SemaphoreType.DMA((n_long, groups, 2)),
            pltpu.SemaphoreType.DMA((groups,)),
            pltpu.SemaphoreType.DMA,
        ],
        compiler_params=pltpu.CompilerParams(
            collective_id=0, has_side_effects=True, vmem_limit_bytes=60 * 1024 * 1024
        ),
    )(queries, keys_values, segment_ids)


def solution(mesh):
    n_long = mesh.shape["ctx"] // 2 + 1
    return jax.shard_map(
        functools.partial(per_device, n_long, mesh.shape["tp"]),
        mesh=mesh,
        in_specs=(
            P(("groups", "dp"), "ctx", "tp"),
            P(("groups", "dp"), None, ("ctx", "tp"), None),
            P(("groups", "dp"), "ctx"),
        ),
        out_specs=P(("groups", "dp"), "ctx", "tp"),
        check_vma=False,
    )
```

```python
import functools
import math

import jax
import jax.numpy as jnp
from jax import lax
from jax.experimental import pallas as pl
from jax.experimental.pallas import tpu as pltpu
from jax.sharding import PartitionSpec as P

HEAD_DIM = 128
MESH = pl.DeviceIdType.MESH
LOG2_SCALE = math.log2(math.e) / math.sqrt(HEAD_DIM)


def kernel(n_long, n_tp, q_ref, kv_ref, seg_ref, out_ref, q_v, seg_v, stage_v, kv_v, bias_v, flip_v, top_v, total_v, sum_v, weights_v, factor_v,
           stage_sem, send_sem, recv_sem, q_sem, seg_sem):
    groups = kv_v.shape[2]
    rows = q_v.shape[0]
    part = kv_ref.shape[2]
    heads = q_v.shape[1] // HEAD_DIM
    per_group = heads // groups
    width = per_group * HEAD_DIM

    c = lax.axis_index("ctx")
    t = lax.axis_index("tp")
    is_long = c < n_long
    first = jnp.where(is_long, 0, c)
    end = jnp.where(is_long, n_long, c + 1)
    own = jnp.where(is_long, c, 0)

    def q_copy(g):
        columns = pl.ds(g * width, width)
        return pltpu.make_async_copy(q_ref.at[0, :, columns], q_v.at[:, columns], q_sem.at[g])

    seg_copy = pltpu.make_async_copy(seg_ref, seg_v, seg_sem)

    def partner(o):
        return lax.rem(t + o, n_tp)

    def place(g, kv):
        return kv_v.at[own, kv, g, pl.ds(pl.multiple_of(t * part, part), part), :]

    def block(tp_index, g, kv):
        column = pl.multiple_of((tp_index * groups + g) * HEAD_DIM, HEAD_DIM)
        return kv_ref.at[0, kv, :, pl.ds(column, HEAD_DIM)]

    def stage_copy(tp_index, g, kv):
        return pltpu.make_async_copy(block(tp_index, g, kv), stage_v.at[kv, g, tp_index], stage_sem.at[kv, g, tp_index])

    def local_copy(g, kv):
        return pltpu.make_async_copy(block(t, g, kv), place(g, kv), recv_sem.at[own, g, kv])

    def remote_copy(dest, distance, o, g, kv):
        return pltpu.make_async_remote_copy(
            src_ref=stage_v.at[kv, g, partner(o)],
            dst_ref=place(g, kv),
            send_sem=send_sem.at[distance, o, g, kv],
            recv_sem=recv_sem.at[own, g, kv],
            device_id={"ctx": dest, "tp": partner(o)},
            device_id_type=MESH,
        )

    barrier = pltpu.get_barrier_semaphore()
    for g in range(groups):
        for kv in range(2):
            for i in range(n_tp):
                stage_copy(i, g, kv).start()
    for o in range(1, n_tp):
        pl.semaphore_signal(barrier, inc=1, device_id={"ctx": c, "tp": partner(o)}, device_id_type=MESH)

    def greet(source, carry):
        for o in range(n_tp):
            pl.semaphore_signal(barrier, inc=1, device_id={"ctx": source, "tp": partner(o)}, device_id_type=MESH)
        return carry

    lax.fori_loop(first, c, greet, 0)
    for g in range(groups):
        for kv in range(2):
            local_copy(g, kv).start()
        q_copy(g).start()
    seg_copy.start()
    for g in range(groups):
        for kv in range(2):
            for i in range(n_tp):
                stage_copy(i, g, kv).wait()
    pl.semaphore_wait(barrier, (end - c) * n_tp - 1)

    for g in range(groups):
        for kv in range(2):
            for o in range(1, n_tp):
                remote_copy(c, 0, o, g, kv).start()
    for g in range(groups):
        for kv in range(2):
            def send(i, carry, g=g, kv=kv):
                dest = c + 1 + i
                for o in range(n_tp):
                    remote_copy(dest, dest - c, o, g, kv).start()
                return carry

            lax.fori_loop(0, end - 1 - c, send, 0)

    seg_copy.wait()
    seg = seg_v[...]
    seg_keys = jnp.transpose(jnp.broadcast_to(seg.astype(jnp.float32), (HEAD_DIM, rows)))[:, :1].astype(jnp.int32)
    key_index = lax.broadcasted_iota(jnp.int32, (rows, rows), 0)
    row_index = lax.broadcasted_iota(jnp.int32, (rows, rows), 1)
    visible = (seg_keys == seg) & (key_index <= row_index)
    bias_v[...] = jnp.where(visible, 0.0, -1e30)

    def arrived(slot, g, kv):
        whole = kv_v.at[slot, kv, g]
        pltpu.make_async_copy(whole, whole, recv_sem.at[slot, g, kv]).wait()

    def scores_of(h, key_rows):
        q = q_v[:, pl.ds(pl.multiple_of(h * HEAD_DIM, HEAD_DIM), HEAD_DIM)]
        return lax.dot_general(key_rows, q, (((1,), (1,)), ((), ())), preferred_element_type=jnp.float32) * LOG2_SCALE

    def close(h, summed):
        out_ref[0, :, h * HEAD_DIM:(h + 1) * HEAD_DIM] = jnp.transpose((summed * (1.0 / total_v[h])).astype(jnp.bfloat16))

    def attend(g, slot, bias, fresh, closing=False):
        key_rows = kv_v[slot, 0, g]
        if fresh:
            flip_v[...] = jnp.transpose(kv_v[slot, 1, g])
        heads_of = [g * per_group + j for j in range(per_group)]

        def add_values(h, weights, factor):
            product = jnp.dot(flip_v[...], weights, preferred_element_type=jnp.float32)
            summed = product if fresh else sum_v[h] * factor + product
            if closing:
                close(h, summed)
            else:
                sum_v[h] = summed

        scores, waiting = scores_of(heads_of[0], key_rows), None
        for j, h in enumerate(heads_of):
            following = scores_of(heads_of[j + 1], key_rows) if j + 1 < per_group else None
            if bias is not None:
                scores = scores + bias[...]
            top = jnp.max(scores, axis=0, keepdims=True)
            factor = None
            if not fresh:
                old = top_v[h]
                top = jnp.maximum(old, top)
                factor = jnp.exp2(old - top)
            weights = jnp.exp2(scores - top)
            total = jnp.sum(weights, axis=0, keepdims=True)
            top_v[h] = top
            total_v[h] = total if fresh else total_v[h] * factor + total
            scores = following
            if not fresh:
                weights_v[j] = weights.astype(jnp.bfloat16)
                factor_v[j] = factor
                continue
            if waiting is not None:
                add_values(*waiting)
            waiting = (h, weights.astype(jnp.bfloat16), factor)
        if fresh:
            add_values(*waiting)
            return
        arrived(slot, g, 1)
        flip_v[...] = jnp.transpose(kv_v[slot, 1, g])
        for j, h in enumerate(heads_of):
            add_values(h, weights_v[j], factor_v[j])

    for g in range(groups):
        q_copy(g).wait()
        arrived(own, g, 0)
        arrived(own, g, 1)
        attend(g, own, bias_v, True)

    for g in range(groups):
        def source_step(i, carry, g=g):
            slot = c - 1 - i
            arrived(slot, g, 0)
            attend(g, slot, None, False)
            return carry

        lax.fori_loop(0, c - first - 1, source_step, 0)

        @pl.when(c > first)
        def _(g=g):
            arrived(first, g, 0)
            attend(g, first, None, False, True)

        @pl.when(c == first)
        def _(g=g):
            for j in range(per_group):
                close(g * per_group + j, sum_v[g * per_group + j])

    for g in range(groups):
        for kv in range(2):
            for o in range(1, n_tp):
                remote_copy(c, 0, o, g, kv).wait_send()

            def sent(i, carry, g=g, kv=kv):
                for o in range(n_tp):
                    remote_copy(c + 1 + i, 1 + i, o, g, kv).wait_send()
                return carry

            lax.fori_loop(0, end - 1 - c, sent, 0)


def per_device(n_long, n_tp, queries, keys_values, segment_ids):
    rows, columns = queries.shape[1:]
    heads = columns // HEAD_DIM
    groups = keys_values.shape[3] // HEAD_DIM // n_tp
    return pl.pallas_call(
        functools.partial(kernel, n_long, n_tp),
        out_shape=pltpu.VMEM(queries.shape, queries.dtype),
        in_specs=[
            pl.BlockSpec(memory_space=pltpu.HBM),
            pl.BlockSpec(memory_space=pltpu.HBM),
            pl.BlockSpec(memory_space=pltpu.HBM),
        ],
        out_specs=pl.BlockSpec(memory_space=pltpu.VMEM),
        scratch_shapes=[
            pltpu.VMEM((rows, columns), jnp.bfloat16),
            pltpu.VMEM((1, rows), jnp.int32),
            pltpu.VMEM((2, groups, n_tp, keys_values.shape[2], HEAD_DIM), jnp.bfloat16),
            pltpu.VMEM((n_long, 2, groups, rows, HEAD_DIM), jnp.bfloat16),
            pltpu.VMEM((rows, rows), jnp.float32),
            pltpu.VMEM((HEAD_DIM, rows), jnp.bfloat16),
            pltpu.VMEM((heads, 1, rows), jnp.float32),
            pltpu.VMEM((heads, 1, rows), jnp.float32),
            pltpu.VMEM((heads, HEAD_DIM, rows), jnp.float32),
            pltpu.VMEM((heads // groups, rows, rows), jnp.bfloat16),
            pltpu.VMEM((heads // groups, 1, rows), jnp.float32),
            pltpu.SemaphoreType.DMA((2, groups, n_tp)),
            pltpu.SemaphoreType.DMA((n_long, n_tp, groups, 2)),
            pltpu.SemaphoreType.DMA((n_long, groups, 2)),
            pltpu.SemaphoreType.DMA((groups,)),
            pltpu.SemaphoreType.DMA,
        ],
        compiler_params=pltpu.CompilerParams(
            collective_id=0, has_side_effects=True, vmem_limit_bytes=60 * 1024 * 1024
        ),
    )(queries, keys_values, segment_ids)


def solution(mesh):
    n_long = mesh.shape["ctx"] // 2 + 1
    return jax.shard_map(
        functools.partial(per_device, n_long, mesh.shape["tp"]),
        mesh=mesh,
        in_specs=(
            P(("groups", "dp"), "ctx", "tp"),
            P(("groups", "dp"), None, ("ctx", "tp"), None),
            P(("groups", "dp"), "ctx"),
        ),
        out_specs=P(("groups", "dp"), "ctx", "tp"),
        check_vma=False,
    )
```
